32 devices in a mesh: seq: 4 (over y, x), expert: 4 (over z), mp: 2 (over core).
Axes of the slice: x: 2, y: 2, z: 4, core: 2. Of those that a mesh axis runs over, the one named last changes fastest.
Arguments:
- activations: bfloat16 [4096, 4096], P('seq', ('expert', 'mp')), may hold values from -6 to 6
- output_gradient: bfloat16 [4096, 4096], P('seq', ('expert', 'mp')), may hold values from -1.5 to 1.5
- input_state_map: bfloat16 [4096, 16], P('seq'), may hold values from -3 to 3
- output_state_map: bfloat16 [4096, 16], P('seq'), may hold values from -3 to 3
- head_decay_speed: float32 [64], P(('expert', 'mp')), may hold values from 1.2207031e-05 to 0.05, as said below
- spike_decay_level: int32 [4096], P('seq'), may hold values from 0 to 2, as said below
- assign: int32 [32], replicated, may hold values from 0 to 15, as said below
- expert_up_weight: bfloat16 [4, 4096, 12288], P('expert', 'mp', 'seq'), may hold values from -0.09375 to 0.09375
- expert_down_weight: bfloat16 [4, 12288, 4096], P('expert', 'seq', 'mp'), may hold values from -0.0546875 to 0.0546875
Outputs:
- grad_x: float32 [4096, 4096], P('seq', ('expert', 'mp'))
- grad_w_up: float32 [4, 4096, 12288], P('expert', 'mp', 'seq')
- grad_w_down: float32 [4, 12288, 4096], P('expert', 'seq', 'mp')
The draws below stay inside these ranges and needn't reach their ends.
Inputs may be any that keep to these rules, and one draw needn't show every extreme that they name: `head_decay_speed`: some of the heads keep a tenth or more of their state over the whole sequence, the others lose it within some tens of tokens. `spike_decay_level`: at most three tokens of the sequence have a nonzero level. `assign`: numbers below 4 are the window's experts: the 8 blocks of one index of seq hold at most one block of each of them, each takes at most 2 blocks in all, and one takes exactly 2.
All inputs are finite; a program needn't handle non-finite values.
Results may differ from the reference program's by a relative error of at most 0.019.
Values may be sent and summed in bfloat16 or wider, within the bound.
A program may use at most 192 MiB of HBM per device.

```python
import math
import jax
import jax.numpy as jnp
from jax import lax

D = 4096
FF = 12288
HEAD = 64
STATE = 16
BLOCK = 128
EXP_ALL = 16
SEQUENCE_TOKENS = 4096
HEADS = 64
EXPERTS = 4
BLOCKS_DEV = 8
SEQ_BLOCKS = 32
SLOTS = 2
N_SEQ = 4
N_MP = 2


def draw_head_decay_speed(key, part):
    key_slow, key_fast, key_pick = jax.random.split(key, 3)
    slow_rate = jax.random.uniform(key_slow, (HEADS,), jnp.float32, math.log(0.05 / SEQUENCE_TOKENS), math.log(0.5 / SEQUENCE_TOKENS))
    fast_rate = jax.random.uniform(key_fast, (HEADS,), jnp.float32, math.log(0.02), math.log(0.05))
    keeping = jax.random.uniform(key_pick, (HEADS,), jnp.float32) < 0.5
    return jnp.exp(jnp.where(keeping, slow_rate, fast_rate)).astype(jnp.float32)


def draw_spike_decay_level(key, part):
    position_random_key, level_random_key = jax.random.split(key, 2)
    spike_positions = jax.random.randint(position_random_key, (3,), 0, SEQUENCE_TOKENS)
    spike_level_list = jax.random.randint(level_random_key, (3,), 1, 3).at[0].set(2)
    return jnp.zeros((SEQUENCE_TOKENS,), jnp.int32).at[spike_positions].max(spike_level_list.astype(jnp.int32))


def draw_assign(key, part):
    key_list = jax.random.split(key, 4)
    route_table = jax.random.randint(key_list[0], (N_SEQ, BLOCKS_DEV), EXPERTS, EXP_ALL).astype(jnp.int32)
    ranking = jax.random.permutation(key_list[1], EXPERTS)
    block_places = jax.vmap(lambda sub_key: jax.random.permutation(sub_key, BLOCKS_DEV))(jax.random.split(key_list[2], N_SEQ))
    shard_keys = jax.random.split(key_list[3], EXPERTS)
    for expert in range(EXPERTS):
        rank_now = jnp.minimum(ranking[expert], 2)
        expert_load = jnp.maximum(1, jnp.right_shift(SLOTS, rank_now))
        shuffled = jax.random.permutation(shard_keys[expert], N_SEQ)
        place_of = jnp.argsort(shuffled)
        is_taken = place_of < expert_load
        marked = is_taken[:, None] & (jnp.arange(BLOCKS_DEV)[None, :] == block_places[:, expert][:, None])
        route_table = jnp.where(marked, expert, route_table)
    return route_table.reshape(SEQ_BLOCKS).astype(jnp.int32)


def shard_levels(rng, shape, cuts, low, top_value):
    level = 1.0
    for dim, blocks in cuts:
        steps = jax.random.uniform(jax.random.fold_in(jax.random.fold_in(rng, 6), dim), (blocks,), jnp.float32, low / len(cuts), top_value / len(cuts))
        level = level * jnp.repeat(jnp.exp(steps), shape[dim] // blocks).reshape((-1,) + (1,) * (len(shape) - 1 - dim))
    return level


def gaussian(rng, shape, deviation, most, pieces=(), held_as=jnp.bfloat16):
    array = jax.random.normal(rng, shape, jnp.float32) * deviation
    if len(pieces) > 0:
        array = shard_levels(rng, shape, pieces, -0.22, 0.18) * array
    return jnp.clip(array, min=-most, max=most).astype(held_as)


def setup_inputs(seed: int = 0) -> dict:
    streams_of = jax.random.split(jax.random.key(seed), 10)
    activations = gaussian(streams_of[0], (SEQUENCE_TOKENS, D), 1.0, 6.0, ((0, 4), (1, 8)))
    output_gradient = gaussian(streams_of[1], (SEQUENCE_TOKENS, D), 0.25, 1.5, ((0, 4), (1, 8)))
    input_state_map = gaussian(streams_of[2], (SEQUENCE_TOKENS, STATE), 0.5, 3.0, ((0, 4),))
    output_state_map = gaussian(streams_of[3], (SEQUENCE_TOKENS, STATE), 0.5, 3.0, ((0, 4),))
    head_decay_speed = draw_head_decay_speed(jax.random.fold_in(streams_of[9], 71), 0)
    spike_decay_level = draw_spike_decay_level(jax.random.fold_in(streams_of[9], 71), 0)
    assign = draw_assign(jax.random.fold_in(streams_of[9], 71), 0)
    expert_up_weight = gaussian(streams_of[7], (EXPERTS, D, FF), D ** -0.5, 0.09375, ((0, 4), (1, 2), (2, 4)))
    expert_down_weight = gaussian(streams_of[8], (EXPERTS, FF, D), FF ** -0.5, 0.0546875, ((0, 4), (1, 4), (2, 2)))
    return dict(activations=activations, output_gradient=output_gradient, input_state_map=input_state_map, output_state_map=output_state_map, head_decay_speed=head_decay_speed, spike_decay_level=spike_decay_level, assign=assign, expert_up_weight=expert_up_weight, expert_down_weight=expert_down_weight)


spike_position_step = 0.3
highest = lax.Precision.HIGHEST

def rounded(rounded_in):
    return lax.optimization_barrier(rounded_in.astype(jnp.bfloat16)).astype(jnp.float32)

def slot_rows(chosen, present, select, blocks):
    position = jnp.argmax(chosen.astype(jnp.int32), axis=1).astype(jnp.int32)
    picked = blocks[jnp.arange(N_SEQ), position].astype(jnp.float32)
    picked = picked * present.astype(jnp.float32)[:, None, None]
    slot_block = jnp.einsum('js,srd->jrd', select, picked, precision=highest)
    return slot_block.astype(jnp.bfloat16).reshape(SLOTS * BLOCK, D)

def reference(activations, output_gradient, input_state_map, output_state_map, head_decay_speed, spike_decay_level, assign, expert_up_weight, expert_down_weight):
    input_scale = jnp.sqrt(1.0 - jnp.exp(-2.0 * head_decay_speed))
    every_spike_level = -head_decay_speed[None, :] - spike_position_step * spike_decay_level.astype(jnp.float32)[:, None]
    factor_all = jnp.exp(every_spike_level)
    b_float = input_state_map.astype(jnp.float32)
    c_float = output_state_map.astype(jnp.float32)
    scaled = activations.astype(jnp.float32).reshape(SEQUENCE_TOKENS, HEADS, HEAD) * input_scale[None, :, None]

    def forward_step(scan_state, step_in):
        decay_factor, x_now, b_now, c_now = step_in
        scan_state = decay_factor[:, None, None] * scan_state + x_now[:, :, None] * b_now[None, None, :]
        return (scan_state, jnp.einsum('hpn,n->hp', scan_state, c_now, precision=highest))
    _, outputs = lax.scan(forward_step, jnp.zeros((HEADS, HEAD, STATE), jnp.float32), (factor_all, scaled, b_float, c_float))
    mixed_out = (activations.astype(jnp.float32) + outputs.reshape(SEQUENCE_TOKENS, D)).astype(jnp.bfloat16)
    route_table = assign.reshape(N_SEQ, BLOCKS_DEV)
    mixed_blocks = mixed_out.reshape(N_SEQ, BLOCKS_DEV, BLOCK, D)
    grad_blocks = output_gradient.reshape(N_SEQ, BLOCKS_DEV, BLOCK, D)
    half_width = D // N_MP
    group_width = FF // N_SEQ
    token_grad = jnp.zeros((N_SEQ, BLOCKS_DEV, BLOCK, D), jnp.float32)
    up_grads = []
    down_grads = []
    for expert in range(EXPERTS):
        chosen = route_table == expert
        present = jnp.any(chosen, axis=1)
        slot_of = jnp.cumsum(present.astype(jnp.int32)) - 1
        select = ((slot_of[None, :] == jnp.arange(SLOTS)[:, None]) & present[None, :]).astype(jnp.float32)
        x_rows = slot_rows(chosen, present, select, mixed_blocks)
        g_rows = slot_rows(chosen, present, select, grad_blocks)
        up_w = expert_up_weight[expert]
        down_w = expert_down_weight[expert]
        pre_act = jnp.zeros((SLOTS * BLOCK, FF), jnp.float32)
        act_grad = jnp.zeros((SLOTS * BLOCK, FF), jnp.float32)
        for part_index in range(N_MP):
            low_index = part_index * half_width
            pre_act = pre_act + rounded(jnp.dot(x_rows[:, low_index:low_index + half_width], up_w[low_index:low_index + half_width], preferred_element_type=jnp.float32))
            act_grad = act_grad + rounded(jnp.dot(g_rows[:, low_index:low_index + half_width], down_w[:, low_index:low_index + half_width].T, preferred_element_type=jnp.float32))
        activation = jax.nn.silu(pre_act).astype(jnp.bfloat16)
        down_grads.append(jnp.dot(activation.T, g_rows, preferred_element_type=jnp.float32))
        sigmoid_pre = jax.nn.sigmoid(pre_act)
        pre_grad = (act_grad * sigmoid_pre * (1.0 + pre_act * (1.0 - sigmoid_pre))).astype(jnp.bfloat16)
        up_grads.append(jnp.dot(x_rows.T, pre_grad, preferred_element_type=jnp.float32))
        row_grad = jnp.zeros((SLOTS * BLOCK, D), jnp.float32)
        for group_index in range(N_SEQ):
            low_index = group_index * group_width
            row_grad = row_grad + rounded(jnp.dot(pre_grad[:, low_index:low_index + group_width], up_w[:, low_index:low_index + group_width].T, preferred_element_type=jnp.float32))
        row_grad = row_grad.astype(jnp.bfloat16).astype(jnp.float32).reshape(SLOTS, BLOCK, D)
        back_rows = jnp.einsum('js,jrd->srd', select, row_grad, precision=highest)
        token_grad = token_grad + chosen.astype(jnp.float32)[:, :, None, None] * back_rows[:, None]
    total_grad = output_gradient.astype(jnp.float32) + token_grad.reshape(SEQUENCE_TOKENS, D)
    grad_view = total_grad.reshape(SEQUENCE_TOKENS, HEADS, HEAD)

    def backward_step(carry, step_in):
        adjoint, factor_next = carry
        decay_factor, grad_now, b_now, c_now = step_in
        adjoint = factor_next[:, None, None] * adjoint + grad_now[:, :, None] * c_now[None, None, :]
        return ((adjoint, decay_factor), jnp.einsum('hpn,n->hp', adjoint, b_now, precision=highest))
    start_carry = (jnp.zeros((HEADS, HEAD, STATE), jnp.float32), jnp.ones((HEADS,), jnp.float32))
    _, scan_grad = lax.scan(backward_step, start_carry, (factor_all, grad_view, b_float, c_float), reverse=True)
    grad_x = total_grad + (input_scale[None, :, None] * scan_grad).reshape(SEQUENCE_TOKENS, D)
    return (grad_x, jnp.stack(up_grads), jnp.stack(down_grads))
```

```python
import functools
import jax
import jax.numpy as jnp
from jax import lax
from jax.experimental import pallas as pl
from jax.experimental.pallas import tpu as pltpu
from jax.sharding import PartitionSpec as P

HEAD = 64
STATE = 16
BLOCK = 128


spike_position_step = 0.3
highest = lax.Precision.HIGHEST


MESH = pl.DeviceIdType.MESH


def place():
    return (lax.axis_index("seq"), lax.axis_index("expert"), lax.axis_index("mp"))


def greet_seq(n_seq, me):
    s, e, m = me
    barrier = pltpu.get_barrier_semaphore()
    for step in range(1, n_seq):
        pl.semaphore_signal(
            barrier, inc=1, device_id=(lax.rem(s + step, n_seq), e, m), device_id_type=MESH
        )
    return barrier


def share_kernel(n_seq, x_ref, out_ref, send_sem, recv_sem):
    s, e, m = place()
    barrier = greet_seq(n_seq, (s, e, m))
    pl.semaphore_wait(barrier, n_seq - 1)
    copies = []
    for step in range(1, n_seq):
        copy = pltpu.make_async_remote_copy(
            src_ref=x_ref,
            dst_ref=out_ref.at[s],
            send_sem=send_sem.at[step],
            recv_sem=recv_sem.at[step],
            device_id=(lax.rem(s + step, n_seq), e, m),
            device_id_type=MESH,
        )
        copy.start()
        copies.append(copy)
    out_ref[s] = x_ref[...]
    for copy in copies:
        copy.wait()


def share(value, n_seq, collective_id):
    return pl.pallas_call(
        functools.partial(share_kernel, n_seq),
        out_shape=jax.ShapeDtypeStruct((n_seq,) + value.shape, value.dtype),
        in_specs=[pl.BlockSpec(memory_space=pltpu.VMEM)],
        out_specs=pl.BlockSpec(memory_space=pltpu.VMEM),
        scratch_shapes=[pltpu.SemaphoreType.DMA((n_seq,)), pltpu.SemaphoreType.DMA((n_seq,))],
        compiler_params=pltpu.CompilerParams(collective_id=collective_id, has_side_effects=True),
    )(value)


def greet_all(n_seq, n_exp, n_mp, me, sources):
    s, e, m = me
    barrier = greet_seq(n_seq, me)
    f = e * n_mp + m
    own_half = f // n_exp == m
    for i in range(n_exp):
        for step in range(n_seq):
            if sources:
                part = m * n_exp + lax.rem(lax.rem(f, n_exp) + i, n_exp)
                device = (lax.rem(s + step, n_seq), part // n_mp, lax.rem(part, n_mp))
            else:
                device = (lax.rem(s + step, n_seq), lax.rem(e + i, n_exp), f // n_exp)
            if i == 0 and step == 0:

                @pl.when(jnp.logical_not(own_half))
                def _():
                    pl.semaphore_signal(barrier, inc=1, device_id=device, device_id_type=MESH)
            else:
                pl.semaphore_signal(barrier, inc=1, device_id=device, device_id_type=MESH)
    pl.semaphore_wait(barrier, n_seq * n_exp + n_seq - 1 - own_half.astype(jnp.int32))


def scatter_copies(n_seq, n_exp, me, device_of, src_of, dst, send_sem, recv_sem, own_half):
    pending = []
    for i in range(n_exp):
        for step in range(n_seq):
            source, device = src_of(i, step), device_of(i, step)
            copy = pltpu.make_async_remote_copy(
                src_ref=source,
                dst_ref=dst,
                send_sem=send_sem.at[i, step],
                recv_sem=recv_sem,
                device_id=device,
                device_id_type=MESH,
            )
            if i == 0 and step == 0:
                local = pltpu.make_async_copy(source, dst, recv_sem)

                @pl.when(own_half)
                def _():
                    local.start()

                @pl.when(jnp.logical_not(own_half))
                def _():
                    copy.start()
            else:
                copy.start()
            pending.append(copy)

    def finish():
        @pl.when(jnp.logical_not(own_half))
        def _():
            pending[0].wait_send()

        for copy in pending[1:]:
            copy.wait_send()

    return finish


def route_kernel(sizes, sel_ref, h_ref, g_ref, hx_ref, gx_ref, h_in, g_in, send_sem, recv_sem, sem_a, sem_b):
    n_seq, n_exp, n_mp, slots = sizes
    me = place()
    s, e, m = me
    f = e * n_mp + m
    own_half = f // n_exp == m
    width = h_ref.shape[-1]
    greet_all(n_seq, n_exp, n_mp, me, True)

    def device_of(i, step):
        return (lax.rem(s + step, n_seq), lax.rem(e + i, n_exp), f // n_exp)

    finishers = []
    for k, (ref, landing) in enumerate(((g_ref, g_in), (h_ref, h_in))):
        finishers.append(
            scatter_copies(
                n_seq,
                n_exp,
                me,
                device_of,
                lambda i, step, ref=ref: ref.at[lax.rem(e + i, n_exp), lax.rem(s + step, n_seq)],
                landing.at[s, lax.rem(f, n_exp)],
                send_sem.at[k],
                recv_sem.at[k],
                own_half,
            )
        )
    copies = []
    for k, (landing, out) in enumerate(((g_in, gx_ref), (h_in, hx_ref))):
        pltpu.make_async_copy(landing, landing, recv_sem.at[k]).wait()
        for j in range(slots):
            for q in range(n_exp):
                total = sel_ref[j, 0] * landing[0, q].astype(jnp.float32)
                for source in range(1, n_seq):
                    total = total + sel_ref[j, source] * landing[source, q].astype(jnp.float32)
                out[s, j, :, q * width : (q + 1) * width] = total.astype(jnp.bfloat16)
        for step in range(1, n_seq):
            copy = pltpu.make_async_remote_copy(
                src_ref=out.at[s],
                dst_ref=out.at[s],
                send_sem=sem_a.at[k, step],
                recv_sem=sem_b.at[k, step],
                device_id=(lax.rem(s + step, n_seq), e, m),
                device_id_type=MESH,
            )
            copy.start()
            copies.append(copy)
    for copy in copies:
        copy.wait()
    for finish in finishers:
        finish()


def route(select, h_pick, g_pick, sizes):
    n_seq, n_exp, n_mp, slots = sizes
    width = h_pick.shape[-1]
    part = BLOCK // n_seq
    picks = [v.reshape(n_exp, n_seq, part, width) for v in (h_pick, g_pick)]
    out = jax.ShapeDtypeStruct((n_seq, slots, part, width * n_exp), jnp.bfloat16)
    vmem = pl.BlockSpec(memory_space=pltpu.VMEM)
    return pl.pallas_call(
        functools.partial(route_kernel, sizes),
        out_shape=(out, out),
        in_specs=[pl.BlockSpec(memory_space=pltpu.SMEM), vmem, vmem],
        out_specs=(vmem, vmem),
        scratch_shapes=[
            pltpu.VMEM((n_seq, n_exp, part, width), jnp.bfloat16),
            pltpu.VMEM((n_seq, n_exp, part, width), jnp.bfloat16),
            pltpu.SemaphoreType.DMA((2, n_exp, n_seq)),
            pltpu.SemaphoreType.DMA((2,)),
            pltpu.SemaphoreType.DMA((2, n_seq)),
            pltpu.SemaphoreType.DMA((2, n_seq)),
        ],
        compiler_params=pltpu.CompilerParams(
            collective_id=1, has_side_effects=True, vmem_limit_bytes=40 * 2**20
        ),
    )(select, *picks)


def unroute_kernel(sizes, sel_ref, r_ref, out_ref, r_in, spread, send_sem, recv_sem, sem_a, sem_b):
    n_seq, n_exp, n_mp, slots = sizes
    me = place()
    s, e, m = me
    f = e * n_mp + m
    own_half = f // n_exp == m
    width = out_ref.shape[-1]
    greet_all(n_seq, n_exp, n_mp, me, False)
    copies = []
    for step in range(1, n_seq):
        target = lax.rem(s + step, n_seq)
        copy = pltpu.make_async_remote_copy(
            src_ref=r_ref.at[target],
            dst_ref=r_in.at[step - 1],
            send_sem=sem_a.at[step],
            recv_sem=sem_b.at[step],
            device_id=(target, e, m),
            device_id_type=MESH,
        )
        copy.start()
        copies.append(copy)
    for copy in copies:
        copy.wait()
    for q in range(n_exp):
        totals = []
        for j in range(slots):
            cut = slice(q * width, (q + 1) * width)
            total = r_ref[s, j, :, cut].astype(jnp.float32)
            for step in range(n_seq - 1):
                total = total + r_in[step, j, :, cut].astype(jnp.float32)
            totals.append(total)
        for source in range(n_seq):
            row = sel_ref[0, source] * totals[0]
            for j in range(1, slots):
                row = row + sel_ref[j, source] * totals[j]
            spread[source, q] = row.astype(jnp.bfloat16)

    def part_of(i):
        return lax.rem(lax.rem(f, n_exp) + i, n_exp)

    def device_of(i, step):
        part = m * n_exp + part_of(i)
        return (lax.rem(s + step, n_seq), part // n_mp, lax.rem(part, n_mp))

    finish = scatter_copies(
        n_seq,
        n_exp,
        me,
        device_of,
        lambda i, step: spread.at[lax.rem(s + step, n_seq), part_of(i)],
        out_ref.at[e, s],
        send_sem,
        recv_sem.at[0],
        own_half,
    )
    pltpu.make_async_copy(out_ref, out_ref, recv_sem.at[0]).wait()
    finish()


def unroute(select, rows, sizes):
    n_seq, n_exp, n_mp, slots = sizes
    part = BLOCK // n_seq
    half_width = rows.shape[-1]
    width = half_width // n_exp
    vmem = pl.BlockSpec(memory_space=pltpu.VMEM)
    return pl.pallas_call(
        functools.partial(unroute_kernel, sizes),
        out_shape=jax.ShapeDtypeStruct((n_exp, n_seq, part, width), jnp.bfloat16),
        in_specs=[pl.BlockSpec(memory_space=pltpu.SMEM), vmem],
        out_specs=vmem,
        scratch_shapes=[
            pltpu.VMEM((n_seq - 1, slots, part, half_width), jnp.bfloat16),
            pltpu.VMEM((n_seq, n_exp, part, width), jnp.bfloat16),
            pltpu.SemaphoreType.DMA((n_exp, n_seq)),
            pltpu.SemaphoreType.DMA((1,)),
            pltpu.SemaphoreType.DMA((n_seq,)),
            pltpu.SemaphoreType.DMA((n_seq,)),
        ],
        compiler_params=pltpu.CompilerParams(
            collective_id=2, has_side_effects=True, vmem_limit_bytes=40 * 2**20
        ),
    )(select, rows.reshape(n_seq, slots, part, half_width))


def swapped(value):
    return lax.ppermute(value, "mp", [(0, 1), (1, 0)])


def split_parts(values):
    high_part = values.astype(jnp.bfloat16)
    low_part = (values - high_part.astype(jnp.float32)).astype(jnp.bfloat16)
    return (high_part, low_part)


def mixing(cum_block, scores, causal):
    spread = cum_block.T[:, :, None] - cum_block.T[:, None, :]
    spread = jnp.where(causal[None], spread, -jnp.inf)
    return jnp.exp(spread) * scores[None]


def per_device(
    activations,
    output_gradient,
    input_state_map,
    output_state_map,
    head_decay_speed,
    spike_decay_level,
    assign,
    expert_up_weight,
    expert_down_weight,
):
    tokens, slice_width = activations.shape
    heads_dev = slice_width // HEAD
    seq_count = lax.axis_size("seq")
    exp_count = lax.axis_size("expert")
    mp_count = lax.axis_size("mp")
    seq_index = lax.axis_index("seq")
    exp_index = lax.axis_index("expert")
    half_width = slice_width * exp_count
    slot_total = seq_count // 2
    input_scale = jnp.sqrt(1.0 - jnp.exp(-2.0 * head_decay_speed))
    row = jnp.arange(tokens)
    spike_count = jnp.dot(
        (row[:, None] >= row[None, :]).astype(jnp.bfloat16),
        spike_decay_level.astype(jnp.bfloat16)[:, None],
        preferred_element_type=jnp.float32,
    )
    cum_level = (
        -(row + 1).astype(jnp.float32)[:, None] * head_decay_speed[None, :]
        - spike_position_step * spike_count
    )
    b_float = input_state_map.astype(jnp.float32)
    c_float = output_state_map.astype(jnp.float32)
    act_heads = activations.reshape(tokens, heads_dev, HEAD)
    scaled = act_heads.astype(jnp.float32) * input_scale[None, :, None]
    span_rows = min(512, tokens)
    span_count = tokens // span_rows
    causal = jnp.arange(span_rows)[:, None] >= jnp.arange(span_rows)[None, :]
    zero_level = jnp.zeros((heads_dev,), jnp.float32)
    carry_state = jnp.zeros((heads_dev, HEAD, STATE), jnp.float32)
    pieces = []
    for position in range(span_count):
        first_row = position * span_rows
        last_row = first_row + span_rows
        cum_block = cum_level[first_row:last_row]
        start_level = cum_level[first_row - 1] if position > 0 else zero_level
        scores = jnp.dot(
            output_state_map[first_row:last_row],
            input_state_map[first_row:last_row].T,
            preferred_element_type=jnp.float32,
        )
        weights = mixing(cum_block, scores, causal)
        weight_high, weight_low = split_parts(weights)
        x_span = act_heads[first_row:last_row]
        inner_part = jnp.einsum(
            "hts,shp->thp", weight_high, x_span, preferred_element_type=jnp.float32
        )
        inner_part = inner_part + jnp.einsum(
            "hts,shp->thp", weight_low, x_span, preferred_element_type=jnp.float32
        )
        inner_part = inner_part * input_scale[None, :, None]
        carried = jnp.exp(cum_block - start_level[None, :])[:, :, None] * jnp.einsum(
            "tn,hpn->thp", c_float[first_row:last_row], carry_state, precision=highest
        )
        pieces.append(inner_part + carried)
        end_level = cum_block[-1]
        tail_decay = jnp.exp(end_level[None, :] - cum_block)
        carry_state = jnp.exp(end_level - start_level)[:, None, None] * carry_state + jnp.einsum(
            "shp,sn->hpn",
            scaled[first_row:last_row] * tail_decay[:, :, None],
            b_float[first_row:last_row],
            precision=highest,
        )
    flat_state = carry_state.reshape(heads_dev, HEAD * STATE)
    spikes = jnp.sum(spike_decay_level).astype(jnp.bfloat16)
    shared = share(
        jnp.concatenate(
            [flat_state.astype(jnp.bfloat16), jnp.full(flat_state.shape, spikes, jnp.bfloat16)], 0
        ),
        seq_count,
        3,
    )
    shard_level = (
        -tokens * head_decay_speed[None, :]
        - spike_position_step * shared[:, heads_dev, 0].astype(jnp.float32)[:, None]
    )
    seq_row = jnp.arange(seq_count)
    reached = (seq_row[:, None] >= seq_row[None, :]).astype(jnp.float32)
    until = jnp.sum(reached[:, :, None] * shard_level[None], axis=1)
    before = until - shard_level
    order = jnp.arange(seq_count)[:, None]
    own_before = lax.dynamic_index_in_dim(before, seq_index, 0)
    own_until = lax.dynamic_index_in_dim(until, seq_index, 0)
    weight_before = jnp.exp(jnp.where(order < seq_index, own_before - until, -jnp.inf))
    weight_after = jnp.exp(jnp.where(order > seq_index, before - own_until, -jnp.inf))
    incoming = jnp.sum(
        weight_before[:, :, None] * shared[:, :heads_dev].astype(jnp.float32), axis=0
    )
    incoming = incoming.reshape(heads_dev, HEAD, STATE)
    outputs = jnp.concatenate(pieces, axis=0) + jnp.exp(cum_level)[:, :, None] * jnp.einsum(
        "tn,hpn->thp", c_float, incoming, precision=highest
    )
    mixed_out = (activations.astype(jnp.float32) + outputs.reshape(tokens, slice_width)).astype(
        jnp.bfloat16
    )
    blocks_dev = tokens // BLOCK
    route_table = assign.reshape(seq_count, blocks_dev)
    own_row = lax.dynamic_index_in_dim(route_table, seq_index, 0, keepdims=False)
    chosen = (own_row[None, :] == jnp.arange(exp_count)[:, None]).astype(jnp.bfloat16)
    h_pick = jnp.einsum(
        "eb,brf->erf",
        chosen,
        mixed_out.reshape(blocks_dev, BLOCK, slice_width),
        preferred_element_type=jnp.float32,
    ).astype(jnp.bfloat16)
    g_pick = jnp.einsum(
        "eb,brf->erf",
        chosen,
        output_gradient.reshape(blocks_dev, BLOCK, slice_width),
        preferred_element_type=jnp.float32,
    ).astype(jnp.bfloat16)
    present = jnp.any(route_table == exp_index, axis=1)
    slot_of = jnp.sum(reached * present.astype(jnp.float32)[None, :], axis=1).astype(jnp.int32) - 1
    select = ((slot_of[None, :] == jnp.arange(slot_total)[:, None]) & present[None, :]).astype(
        jnp.float32
    )
    sizes = (seq_count, exp_count, mp_count, slot_total)
    x_rows, g_rows = route(select, h_pick, g_pick, sizes)
    x_rows = x_rows.reshape(-1, half_width)
    g_rows = g_rows.reshape(-1, half_width)
    up_local = expert_up_weight[0]
    down_local = expert_down_weight[0]
    pre_part = jnp.dot(x_rows, up_local, preferred_element_type=jnp.float32).astype(jnp.bfloat16)
    act_part = jnp.einsum(
        "td,fd->tf", g_rows, down_local, preferred_element_type=jnp.float32
    ).astype(jnp.bfloat16)
    pre_act = pre_part.astype(jnp.float32) + swapped(pre_part).astype(jnp.float32)
    activation = jax.nn.silu(pre_act).astype(jnp.bfloat16)
    down_grad = jnp.einsum("tf,td->fd", activation, g_rows, preferred_element_type=jnp.float32)
    act_grad = act_part.astype(jnp.float32) + swapped(act_part).astype(jnp.float32)
    sigmoid_pre = jax.nn.sigmoid(pre_act)
    pre_grad = (act_grad * sigmoid_pre * (1.0 + pre_act * (1.0 - sigmoid_pre))).astype(jnp.bfloat16)
    up_grad = jnp.einsum("td,tf->df", x_rows, pre_grad, preferred_element_type=jnp.float32)
    row_grad = jnp.einsum("tf,df->td", pre_grad, up_local, preferred_element_type=jnp.float32)
    returned = unroute(select, row_grad.astype(jnp.bfloat16), sizes).reshape(
        exp_count, BLOCK, slice_width
    )
    token_grad = jnp.einsum("eb,erf->brf", chosen, returned, preferred_element_type=jnp.float32)
    total_grad = output_gradient.astype(jnp.float32) + token_grad.reshape(tokens, slice_width)
    grad_view = total_grad.reshape(tokens, heads_dev, HEAD)
    adjoint = jnp.zeros((heads_dev, HEAD, STATE), jnp.float32)
    back_pieces = [None] * span_count
    for position in reversed(range(span_count)):
        first_row = position * span_rows
        last_row = first_row + span_rows
        cum_block = cum_level[first_row:last_row]
        start_level = cum_level[first_row - 1] if position > 0 else zero_level
        scores = jnp.dot(
            output_state_map[first_row:last_row],
            input_state_map[first_row:last_row].T,
            preferred_element_type=jnp.float32,
        )
        weights = mixing(cum_block, scores, causal)
        weight_high, weight_low = split_parts(weights)
        grad_high, grad_low = split_parts(grad_view[first_row:last_row])
        inner_part = jnp.einsum(
            "hts,thp->shp", weight_high, grad_high, preferred_element_type=jnp.float32
        )
        inner_part = inner_part + jnp.einsum(
            "hts,thp->shp", weight_high, grad_low, preferred_element_type=jnp.float32
        )
        inner_part = inner_part + jnp.einsum(
            "hts,thp->shp", weight_low, grad_high, preferred_element_type=jnp.float32
        )
        end_level = cum_block[-1]
        tail_decay = jnp.exp(end_level[None, :] - cum_block)
        carried = tail_decay[:, :, None] * jnp.einsum(
            "sn,hpn->shp", b_float[first_row:last_row], adjoint, precision=highest
        )
        back_pieces[position] = inner_part + carried
        lead_decay = jnp.exp(cum_block - start_level[None, :])
        adjoint = jnp.exp(end_level - start_level)[:, None, None] * adjoint + jnp.einsum(
            "rhp,rn->hpn",
            grad_view[first_row:last_row] * lead_decay[:, :, None],
            c_float[first_row:last_row],
            precision=highest,
        )
    flat_adjoint = adjoint.reshape(heads_dev, HEAD * STATE)

    shared_adjoint = share(
        jnp.concatenate([flat_adjoint, jnp.zeros_like(flat_adjoint)], 0).astype(jnp.bfloat16),
        seq_count,
        4,
    )
    later_adjoint = jnp.sum(
        weight_after[:, :, None] * shared_adjoint[:, :heads_dev].astype(jnp.float32), axis=0
    )
    later_adjoint = later_adjoint.reshape(heads_dev, HEAD, STATE)
    scan_grad = jnp.concatenate(back_pieces, axis=0) + jnp.exp(cum_level[-1][None, :] - cum_level)[
        :, :, None
    ] * jnp.einsum("sn,hpn->shp", b_float, later_adjoint, precision=highest)
    grad_x = total_grad + (input_scale[None, :, None] * scan_grad).reshape(tokens, slice_width)
    return (grad_x, up_grad[None], down_grad[None])


def solution(mesh):
    in_specs = (
        P("seq", ("expert", "mp")),
        P("seq", ("expert", "mp")),
        P("seq", None),
        P("seq", None),
        P(("expert", "mp")),
        P("seq"),
        P(),
        P("expert", "mp", "seq"),
        P("expert", "seq", "mp"),
    )
    out_specs = (P("seq", ("expert", "mp")), P("expert", "mp", "seq"), P("expert", "seq", "mp"))
    return jax.shard_map(
        per_device, mesh=mesh, in_specs=in_specs, out_specs=out_specs, check_vma=False
    )
```

```python
import functools
import jax
import jax.numpy as jnp
from jax import lax
from jax.experimental import pallas as pl
from jax.experimental.pallas import tpu as pltpu
from jax.sharding import PartitionSpec as P

HEAD = 64
STATE = 16
BLOCK = 128


spike_position_step = 0.3


MESH = pl.DeviceIdType.MESH


def place():
    return (lax.axis_index("seq"), lax.axis_index("expert"), lax.axis_index("mp"))


def greet_seq(n_seq, me):
    s, e, m = me
    barrier = pltpu.get_barrier_semaphore()
    for step in range(1, n_seq):
        pl.semaphore_signal(
            barrier, inc=1, device_id=(lax.rem(s + step, n_seq), e, m), device_id_type=MESH
        )
    return barrier


def share_kernel(n_seq, x_ref, out_ref, send_sem, recv_sem):
    s, e, m = place()
    barrier = greet_seq(n_seq, (s, e, m))
    pl.semaphore_wait(barrier, n_seq - 1)
    copies = []
    for step in range(1, n_seq):
        copy = pltpu.make_async_remote_copy(
            src_ref=x_ref,
            dst_ref=out_ref.at[s],
            send_sem=send_sem.at[step],
            recv_sem=recv_sem.at[step],
            device_id=(lax.rem(s + step, n_seq), e, m),
            device_id_type=MESH,
        )
        copy.start()
        copies.append(copy)
    out_ref[s] = x_ref[...]
    for copy in copies:
        copy.wait()


def share(value, n_seq, collective_id):
    return pl.pallas_call(
        functools.partial(share_kernel, n_seq),
        out_shape=jax.ShapeDtypeStruct((n_seq,) + value.shape, value.dtype),
        in_specs=[pl.BlockSpec(memory_space=pltpu.VMEM)],
        out_specs=pl.BlockSpec(memory_space=pltpu.VMEM),
        scratch_shapes=[pltpu.SemaphoreType.DMA((n_seq,)), pltpu.SemaphoreType.DMA((n_seq,))],
        compiler_params=pltpu.CompilerParams(collective_id=collective_id, has_side_effects=True),
    )(value)


def greet_all(n_seq, n_exp, n_mp, me, sources):
    s, e, m = me
    barrier = greet_seq(n_seq, me)
    f = e * n_mp + m
    own_half = f // n_exp == m
    for i in range(n_exp):
        for step in range(n_seq):
            if sources:
                part = m * n_exp + lax.rem(lax.rem(f, n_exp) + i, n_exp)
                device = (lax.rem(s + step, n_seq), part // n_mp, lax.rem(part, n_mp))
            else:
                device = (lax.rem(s + step, n_seq), lax.rem(e + i, n_exp), f // n_exp)
            if i == 0 and step == 0:

                @pl.when(jnp.logical_not(own_half))
                def _():
                    pl.semaphore_signal(barrier, inc=1, device_id=device, device_id_type=MESH)
            else:
                pl.semaphore_signal(barrier, inc=1, device_id=device, device_id_type=MESH)
    pl.semaphore_wait(barrier, n_seq * n_exp + n_seq - 1 - own_half.astype(jnp.int32))


def scatter_copies(n_seq, n_exp, me, device_of, src_of, dst, send_sem, recv_sem, own_half):
    pending = []
    for i in range(n_exp):
        for step in range(n_seq):
            source, device = src_of(i, step), device_of(i, step)
            copy = pltpu.make_async_remote_copy(
                src_ref=source,
                dst_ref=dst,
                send_sem=send_sem.at[i, step],
                recv_sem=recv_sem,
                device_id=device,
                device_id_type=MESH,
            )
            if i == 0 and step == 0:
                local = pltpu.make_async_copy(source, dst, recv_sem)

                @pl.when(own_half)
                def _():
                    local.start()

                @pl.when(jnp.logical_not(own_half))
                def _():
                    copy.start()
            else:
                copy.start()
            pending.append(copy)

    def finish():
        @pl.when(jnp.logical_not(own_half))
        def _():
            pending[0].wait_send()

        for copy in pending[1:]:
            copy.wait_send()

    return finish


def route_kernel(sizes, sel_ref, h_ref, g_ref, hx_ref, gx_ref, h_in, g_in, send_sem, recv_sem, sem_a, sem_b):
    n_seq, n_exp, n_mp, slots = sizes
    me = place()
    s, e, m = me
    f = e * n_mp + m
    own_half = f // n_exp == m
    width = h_ref.shape[-1]
    greet_all(n_seq, n_exp, n_mp, me, True)

    def device_of(i, step):
        return (lax.rem(s + step, n_seq), lax.rem(e + i, n_exp), f // n_exp)

    finishers = []
    for k, (ref, landing) in enumerate(((g_ref, g_in), (h_ref, h_in))):
        finishers.append(
            scatter_copies(
                n_seq,
                n_exp,
                me,
                device_of,
                lambda i, step, ref=ref: ref.at[lax.rem(e + i, n_exp), lax.rem(s + step, n_seq)],
                landing.at[s, lax.rem(f, n_exp)],
                send_sem.at[k],
                recv_sem.at[k],
                own_half,
            )
        )
    copies = []
    for k, (landing, out) in enumerate(((g_in, gx_ref), (h_in, hx_ref))):
        pltpu.make_async_copy(landing, landing, recv_sem.at[k]).wait()
        for j in range(slots):
            for q in range(n_exp):
                total = sel_ref[j, 0] * landing[0, q].astype(jnp.float32)
                for source in range(1, n_seq):
                    total = total + sel_ref[j, source] * landing[source, q].astype(jnp.float32)
                out[s, j, :, q * width : (q + 1) * width] = total.astype(jnp.bfloat16)
        for step in range(1, n_seq):
            copy = pltpu.make_async_remote_copy(
                src_ref=out.at[s],
                dst_ref=out.at[s],
                send_sem=sem_a.at[k, step],
                recv_sem=sem_b.at[k, step],
                device_id=(lax.rem(s + step, n_seq), e, m),
                device_id_type=MESH,
            )
            copy.start()
            copies.append(copy)
    for copy in copies:
        copy.wait()
    for finish in finishers:
        finish()


def route(select, h_pick, g_pick, sizes):
    n_seq, n_exp, n_mp, slots = sizes
    width = h_pick.shape[-1]
    part = BLOCK // n_seq
    picks = [v.reshape(n_exp, n_seq, part, width) for v in (h_pick, g_pick)]
    out = jax.ShapeDtypeStruct((n_seq, slots, part, width * n_exp), jnp.bfloat16)
    vmem = pl.BlockSpec(memory_space=pltpu.VMEM)
    return pl.pallas_call(
        functools.partial(route_kernel, sizes),
        out_shape=(out, out),
        in_specs=[pl.BlockSpec(memory_space=pltpu.SMEM), vmem, vmem],
        out_specs=(vmem, vmem),
        scratch_shapes=[
            pltpu.VMEM((n_seq, n_exp, part, width), jnp.bfloat16),
            pltpu.VMEM((n_seq, n_exp, part, width), jnp.bfloat16),
            pltpu.SemaphoreType.DMA((2, n_exp, n_seq)),
            pltpu.SemaphoreType.DMA((2,)),
            pltpu.SemaphoreType.DMA((2, n_seq)),
            pltpu.SemaphoreType.DMA((2, n_seq)),
        ],
        compiler_params=pltpu.CompilerParams(
            collective_id=1, has_side_effects=True, vmem_limit_bytes=40 * 2**20
        ),
    )(select, *picks)


def unroute_kernel(sizes, sel_ref, r_ref, out_ref, r_in, spread, send_sem, recv_sem, sem_a, sem_b):
    n_seq, n_exp, n_mp, slots = sizes
    me = place()
    s, e, m = me
    f = e * n_mp + m
    own_half = f // n_exp == m
    width = out_ref.shape[-1]
    greet_all(n_seq, n_exp, n_mp, me, False)
    copies = []
    for step in range(1, n_seq):
        target = lax.rem(s + step, n_seq)
        copy = pltpu.make_async_remote_copy(
            src_ref=r_ref.at[target],
            dst_ref=r_in.at[step - 1],
            send_sem=sem_a.at[step],
            recv_sem=sem_b.at[step],
            device_id=(target, e, m),
            device_id_type=MESH,
        )
        copy.start()
        copies.append(copy)
    for copy in copies:
        copy.wait()
    for q in range(n_exp):
        totals = []
        for j in range(slots):
            cut = slice(q * width, (q + 1) * width)
            total = r_ref[s, j, :, cut].astype(jnp.float32)
            for step in range(n_seq - 1):
                total = total + r_in[step, j, :, cut].astype(jnp.float32)
            totals.append(total)
        for source in range(n_seq):
            row = sel_ref[0, source] * totals[0]
            for j in range(1, slots):
                row = row + sel_ref[j, source] * totals[j]
            spread[source, q] = row.astype(jnp.bfloat16)

    def part_of(i):
        return lax.rem(lax.rem(f, n_exp) + i, n_exp)

    def device_of(i, step):
        part = m * n_exp + part_of(i)
        return (lax.rem(s + step, n_seq), part // n_mp, lax.rem(part, n_mp))

    finish = scatter_copies(
        n_seq,
        n_exp,
        me,
        device_of,
        lambda i, step: spread.at[lax.rem(s + step, n_seq), part_of(i)],
        out_ref.at[e, s],
        send_sem,
        recv_sem.at[0],
        own_half,
    )
    pltpu.make_async_copy(out_ref, out_ref, recv_sem.at[0]).wait()
    finish()


def unroute(select, rows, sizes):
    n_seq, n_exp, n_mp, slots = sizes
    part = BLOCK // n_seq
    half_width = rows.shape[-1]
    width = half_width // n_exp
    vmem = pl.BlockSpec(memory_space=pltpu.VMEM)
    return pl.pallas_call(
        functools.partial(unroute_kernel, sizes),
        out_shape=jax.ShapeDtypeStruct((n_exp, n_seq, part, width), jnp.bfloat16),
        in_specs=[pl.BlockSpec(memory_space=pltpu.SMEM), vmem],
        out_specs=vmem,
        scratch_shapes=[
            pltpu.VMEM((n_seq - 1, slots, part, half_width), jnp.bfloat16),
            pltpu.VMEM((n_seq, n_exp, part, width), jnp.bfloat16),
            pltpu.SemaphoreType.DMA((n_exp, n_seq)),
            pltpu.SemaphoreType.DMA((1,)),
            pltpu.SemaphoreType.DMA((n_seq,)),
            pltpu.SemaphoreType.DMA((n_seq,)),
        ],
        compiler_params=pltpu.CompilerParams(
            collective_id=2, has_side_effects=True, vmem_limit_bytes=40 * 2**20
        ),
    )(select, rows.reshape(n_seq, slots, part, half_width))


def swapped(value):
    return lax.ppermute(value, "mp", [(0, 1), (1, 0)])


def contract(left, right, left_dim, right_dim):
    return lax.dot_general(
        left, right, (((left_dim,), (right_dim,)), ((), ())), preferred_element_type=jnp.float32
    )


def scan_kernel(reverse, speed_ref, x_ref, b_ref, c_ref, wide_ref, col_ref, row_ref, y_ref, state_ref):
    blocks = x_ref.shape[0] // BLOCK
    width = x_ref.shape[1]
    step = lax.broadcasted_iota(jnp.int32, (BLOCK, 1), 0).astype(jnp.float32) + 1.0
    later = lax.broadcasted_iota(jnp.int32, (BLOCK, BLOCK), 0)
    earlier = lax.broadcasted_iota(jnp.int32, (BLOCK, BLOCK), 1)
    causal = later >= earlier
    gap = (later - earlier).astype(jnp.float32)
    left_lane = lax.broadcasted_iota(jnp.int32, (BLOCK, 2 * HEAD), 1) < HEAD
    state = jnp.zeros(state_ref.shape, jnp.float32)
    for k in reversed(range(blocks)) if reverse else range(blocks):
        rows = slice(k * BLOCK, (k + 1) * BLOCK)
        spikes = col_ref[rows]
        if k > 0:
            since = spikes - col_ref[k * BLOCK - 1 : k * BLOCK]
        else:
            since = spikes
        level = -step * wide_ref[...] - spike_position_step * since
        end = level[BLOCK - 1 :]
        b_now, c_now = b_ref[rows], c_ref[rows]
        scores = contract(c_now, b_now, 1, 1)
        spike_gap = spike_position_step * (spikes - row_ref[k : k + 1])
        x_now = x_ref[rows].astype(jnp.float32)
        from_start, to_end = jnp.exp(level), jnp.exp(end - level)
        held = state.astype(jnp.bfloat16)
        if reverse:
            carried = to_end * contract(b_now, held, 1, 0)
            added = contract(c_now, (x_now * from_start).astype(jnp.bfloat16), 0, 0)
        else:
            carried = from_start * contract(c_now, held, 1, 0)
            added = contract(b_now, (x_now * to_end).astype(jnp.bfloat16), 0, 0)
        state = jnp.exp(end) * state + added
        for pair in range(width // (2 * HEAD)):
            lanes = slice(pair * 2 * HEAD, (pair + 1) * 2 * HEAD)
            x_pair = x_ref[rows, lanes].astype(jnp.bfloat16)
            parts = []
            for head in (2 * pair, 2 * pair + 1):
                spread = jnp.where(causal, -gap * speed_ref[head] - spike_gap, -jnp.inf)
                weights = (jnp.exp(spread) * scores).astype(jnp.bfloat16)
                parts.append(contract(weights, x_pair, 0 if reverse else 1, 0))
            y_ref[rows, lanes] = carried[:, lanes] + jnp.where(left_lane, parts[0], parts[1])
    state_ref[...] = state


def local_scan(reverse, speed, x, b, c, spike_count):
    tokens, width = x.shape
    vmem = pl.BlockSpec(memory_space=pltpu.VMEM)
    return pl.pallas_call(
        functools.partial(scan_kernel, reverse),
        out_shape=(
            jax.ShapeDtypeStruct((tokens, width), jnp.float32),
            jax.ShapeDtypeStruct((STATE, width), jnp.float32),
        ),
        in_specs=[pl.BlockSpec(memory_space=pltpu.SMEM)] + [vmem] * 6,
        out_specs=(vmem, vmem),
        compiler_params=pltpu.CompilerParams(vmem_limit_bytes=40 * 2**20),
    )(
        speed,
        x,
        b,
        c,
        jnp.repeat(speed, HEAD)[None, :],
        spike_count,
        spike_count.reshape(tokens // BLOCK, BLOCK),
    )


def per_device(
    activations,
    output_gradient,
    input_state_map,
    output_state_map,
    head_decay_speed,
    spike_decay_level,
    assign,
    expert_up_weight,
    expert_down_weight,
):
    tokens, slice_width = activations.shape
    seq_count = lax.axis_size("seq")
    exp_count = lax.axis_size("expert")
    mp_count = lax.axis_size("mp")
    seq_index = lax.axis_index("seq")
    exp_index = lax.axis_index("expert")
    half_width = slice_width * exp_count
    slot_total = seq_count // 2
    input_scale = jnp.sqrt(1.0 - jnp.exp(-2.0 * head_decay_speed))
    row = jnp.arange(tokens)
    spike_count = jnp.dot(
        (row[:, None] >= row[None, :]).astype(jnp.bfloat16),
        spike_decay_level.astype(jnp.bfloat16)[:, None],
        preferred_element_type=jnp.float32,
    )
    wide_speed = jnp.repeat(head_decay_speed, HEAD)[None, :]
    wide_scale = jnp.repeat(input_scale, HEAD)[None, :]
    cum_level = (
        -(row + 1).astype(jnp.float32)[:, None] * wide_speed - spike_position_step * spike_count
    )
    scan_local, flat_state = local_scan(
        False, head_decay_speed, activations, input_state_map, output_state_map, spike_count
    )
    spikes = jnp.sum(spike_decay_level).astype(jnp.bfloat16)
    shared = share(
        jnp.concatenate(
            [flat_state.astype(jnp.bfloat16), jnp.full(flat_state.shape, spikes, jnp.bfloat16)], 0
        ),
        seq_count,
        3,
    )
    shard_level = (
        -tokens * wide_speed
        - spike_position_step * shared[:, STATE, 0].astype(jnp.float32)[:, None]
    )
    seq_row = jnp.arange(seq_count)
    reached = (seq_row[:, None] >= seq_row[None, :]).astype(jnp.float32)
    until = jnp.sum(reached[:, :, None] * shard_level[None], axis=1)
    before = until - shard_level
    order = jnp.arange(seq_count)[:, None]
    own_before = lax.dynamic_index_in_dim(before, seq_index, 0)
    own_until = lax.dynamic_index_in_dim(until, seq_index, 0)
    weight_before = jnp.exp(jnp.where(order < seq_index, own_before - until, -jnp.inf))
    weight_after = jnp.exp(jnp.where(order > seq_index, before - own_until, -jnp.inf))
    incoming = jnp.sum(
        weight_before[:, None, :] * shared[:, :STATE].astype(jnp.float32), axis=0
    )
    outputs = scan_local + jnp.exp(cum_level) * jnp.dot(
        output_state_map, incoming.astype(jnp.bfloat16), preferred_element_type=jnp.float32
    )
    mixed_out = (activations.astype(jnp.float32) + wide_scale * outputs).astype(jnp.bfloat16)
    blocks_dev = tokens // BLOCK
    route_table = assign.reshape(seq_count, blocks_dev)
    own_row = lax.dynamic_index_in_dim(route_table, seq_index, 0, keepdims=False)
    chosen = (own_row[None, :] == jnp.arange(exp_count)[:, None]).astype(jnp.bfloat16)
    h_pick = jnp.einsum(
        "eb,brf->erf",
        chosen,
        mixed_out.reshape(blocks_dev, BLOCK, slice_width),
        preferred_element_type=jnp.float32,
    ).astype(jnp.bfloat16)
    g_pick = jnp.einsum(
        "eb,brf->erf",
        chosen,
        output_gradient.reshape(blocks_dev, BLOCK, slice_width),
        preferred_element_type=jnp.float32,
    ).astype(jnp.bfloat16)
    present = jnp.any(route_table == exp_index, axis=1)
    slot_of = jnp.sum(reached * present.astype(jnp.float32)[None, :], axis=1).astype(jnp.int32) - 1
    select = ((slot_of[None, :] == jnp.arange(slot_total)[:, None]) & present[None, :]).astype(
        jnp.float32
    )
    sizes = (seq_count, exp_count, mp_count, slot_total)
    x_rows, g_rows = route(select, h_pick, g_pick, sizes)
    x_rows = x_rows.reshape(-1, half_width)
    g_rows = g_rows.reshape(-1, half_width)
    up_local = expert_up_weight[0]
    down_local = expert_down_weight[0]
    pre_part = jnp.dot(x_rows, up_local, preferred_element_type=jnp.float32).astype(jnp.bfloat16)
    act_part = jnp.einsum(
        "td,fd->tf", g_rows, down_local, preferred_element_type=jnp.float32
    ).astype(jnp.bfloat16)
    pre_act = pre_part.astype(jnp.float32) + swapped(pre_part).astype(jnp.float32)
    activation = jax.nn.silu(pre_act).astype(jnp.bfloat16)
    down_grad = jnp.einsum("tf,td->fd", activation, g_rows, preferred_element_type=jnp.float32)
    act_grad = act_part.astype(jnp.float32) + swapped(act_part).astype(jnp.float32)
    sigmoid_pre = jax.nn.sigmoid(pre_act)
    pre_grad = (act_grad * sigmoid_pre * (1.0 + pre_act * (1.0 - sigmoid_pre))).astype(jnp.bfloat16)
    up_grad = jnp.einsum("td,tf->df", x_rows, pre_grad, preferred_element_type=jnp.float32)
    row_grad = jnp.einsum("tf,df->td", pre_grad, up_local, preferred_element_type=jnp.float32)
    returned = unroute(select, row_grad.astype(jnp.bfloat16), sizes).reshape(
        exp_count, BLOCK, slice_width
    )
    token_grad = jnp.einsum("eb,erf->brf", chosen, returned, preferred_element_type=jnp.float32)
    total_grad = output_gradient.astype(jnp.float32) + token_grad.reshape(tokens, slice_width)
    adjoint_local, flat_adjoint = local_scan(
        True, head_decay_speed, total_grad, input_state_map, output_state_map, spike_count
    )
    shared_adjoint = share(
        flat_adjoint.astype(jnp.bfloat16),
        seq_count,
        4,
    )
    later_adjoint = jnp.sum(
        weight_after[:, None, :] * shared_adjoint.astype(jnp.float32), axis=0
    )
    scan_grad = adjoint_local + jnp.exp(cum_level[-1:] - cum_level) * jnp.dot(
        input_state_map, later_adjoint.astype(jnp.bfloat16), preferred_element_type=jnp.float32
    )
    grad_x = total_grad + wide_scale * scan_grad
    return (grad_x, up_grad[None], down_grad[None])


def solution(mesh):
    in_specs = (
        P("seq", ("expert", "mp")),
        P("seq", ("expert", "mp")),
        P("seq", None),
        P("seq", None),
        P(("expert", "mp")),
        P("seq"),
        P(),
        P("expert", "mp", "seq"),
        P("expert", "seq", "mp"),
    )
    out_specs = (P("seq", ("expert", "mp")), P("expert", "mp", "seq"), P("expert", "seq", "mp"))
    return jax.shard_map(
        per_device, mesh=mesh, in_specs=in_specs, out_specs=out_specs, check_vma=False
    )
```
